256 devices in a mesh: row: 16 (over y, z_lo, core), col: 16 (over z_hi, x).
Axes of the slice: x: 4, y: 4, z: 8 (z_hi: 4, z_lo: 2; z = z_hi * 2 + z_lo), core: 2. Of those that a mesh axis runs over, the one named last changes fastest.
Arguments:
- tokens: bfloat16 [2048, 6144], P('col', 'row'), may hold values from -6 to 6
- up_weight: bfloat16 [6144, 24576], P('row', 'col'), may hold values from -0.078125 to 0.078125
- down_weight: bfloat16 [24576, 6144], P('col', 'row'), may hold values from -0.0390625 to 0.0390625
- cotangent: bfloat16 [2048, 6144], P('col', 'row'), may hold values from -6 to 6
Outputs:
- branch_out: bfloat16 [2048, 6144], P('col', 'row')
- token_grad: bfloat16 [2048, 6144], P('col', 'row')
- up_grad: float32 [6144, 24576], P('row', 'col')
- down_grad: float32 [24576, 6144], P('col', 'row')
The draws below stay inside these ranges and needn't reach their ends.
All inputs are finite; a program needn't handle non-finite values.
Results may differ from the reference program's by a relative error of at most 0.033.
Values may be sent and summed in bfloat16 or wider, within the bound.
No kernel may reach another device: no remote copies, remote signals or barrier semaphores. Data moves between devices by JAX's collectives and lax.ppermute only.
A program may use at most 128 MiB of HBM per device.

```python
import jax
import jax.numpy as jnp
from jax import lax

D = 6144
FF = 24576
TOKENS = 2048
ROW_WIDTH = 384
HID_COL = 1536
N_ROW = 16
N_COL = 16


def block_scale(stream_key, dims, split, smallest, top_value):
    def one(axis_at, shards_of):
        steps = jax.random.uniform(jax.random.fold_in(jax.random.fold_in(stream_key, 6), axis_at), (shards_of,), jnp.float32, smallest / len(split), top_value / len(split))
        return jnp.repeat(jnp.exp(steps), dims[axis_at] // shards_of).reshape((-1,) + (1,) * (len(dims) - axis_at - 1))

    factor_of = one(*split[0])
    for cut in split[1:]:
        factor_of = factor_of * one(*cut)
    return factor_of


def scatter_about(rng, shape, scale, reach, pieces=(), kind=jnp.bfloat16):
    factor_of = block_scale(rng, shape, pieces, -0.22, 0.18) if pieces else 1.0
    result = jax.random.normal(rng, shape, jnp.float32) * scale * factor_of
    return jnp.minimum(jnp.maximum(result, -reach), reach).astype(kind)


def setup_inputs(seed: int = 0) -> dict:
    splits = jax.random.split(jax.random.key(seed), 5)
    tokens = scatter_about(splits[0], (TOKENS, D), 1.0, 6.0, ((0, 16), (1, 16)))
    up_weight = scatter_about(splits[1], (D, FF), D ** -0.5, 0.078125, ((0, 16), (1, 16)))
    down_weight = scatter_about(splits[2], (FF, D), FF ** -0.5, 0.0390625, ((0, 16), (1, 16)))
    cotangent = scatter_about(splits[3], (TOKENS, D), 1.0, 6.0, ((0, 16), (1, 16)))
    return dict(tokens=tokens, up_weight=up_weight, down_weight=down_weight, cotangent=cotangent)


SQRT_TWO_OVER_PI = 0.7978845608028654
CUBIC = 0.044715


def gelu_value(pre):
    inner = jnp.tanh(SQRT_TWO_OVER_PI * (pre + CUBIC * pre * pre * pre))
    return 0.5 * pre * (1.0 + inner)


def gelu_slope(pre):
    inner = jnp.tanh(SQRT_TWO_OVER_PI * (pre + CUBIC * pre * pre * pre))
    return 0.5 * (1.0 + inner) + 0.5 * pre * (1.0 - inner * inner) * SQRT_TWO_OVER_PI * (1.0 + 3.0 * CUBIC * pre * pre)


def rounded(term):
    return lax.optimization_barrier(term.astype(jnp.bfloat16)).astype(jnp.float32)


def reference(tokens, up_weight, down_weight, cotangent):
    contract_last = (((1,), (1,)), ((), ()))
    pre = jnp.zeros((TOKENS, FF), jnp.float32)
    for block in range(N_ROW):
        lower = block * ROW_WIDTH
        term = jnp.dot(tokens[:, lower:lower + ROW_WIDTH], up_weight[lower:lower + ROW_WIDTH, :], preferred_element_type=jnp.float32)
        pre = pre + rounded(term)
    hidden = gelu_value(pre).astype(jnp.bfloat16)
    summed = jnp.zeros((TOKENS, D), jnp.float32)
    for block in range(N_COL):
        lower = block * HID_COL
        term = jnp.dot(hidden[:, lower:lower + HID_COL], down_weight[lower:lower + HID_COL, :], preferred_element_type=jnp.float32)
        summed = summed + rounded(term)
    branch_out = summed.astype(jnp.bfloat16)
    grad_pre = jnp.zeros((TOKENS, FF), jnp.float32)
    for block in range(N_ROW):
        lower = block * ROW_WIDTH
        term = lax.dot_general(cotangent[:, lower:lower + ROW_WIDTH], down_weight[:, lower:lower + ROW_WIDTH], contract_last, preferred_element_type=jnp.float32)
        grad_pre = grad_pre + rounded(term)
    hidden_grad = (grad_pre * gelu_slope(pre)).astype(jnp.bfloat16)
    back_sum = jnp.zeros((TOKENS, D), jnp.float32)
    for block in range(N_COL):
        lower = block * HID_COL
        term = lax.dot_general(hidden_grad[:, lower:lower + HID_COL], up_weight[:, lower:lower + HID_COL], contract_last, preferred_element_type=jnp.float32)
        back_sum = back_sum + rounded(term)
    token_grad = back_sum.astype(jnp.bfloat16)
    contract_first = (((0,), (0,)), ((), ()))
    up_grad = lax.dot_general(tokens, hidden_grad, contract_first, preferred_element_type=jnp.float32)
    down_grad = lax.dot_general(hidden, cotangent, contract_first, preferred_element_type=jnp.float32)
    return (branch_out, token_grad, up_grad, down_grad)
```

```python
import jax
import jax.numpy as jnp
from jax import lax
from jax.sharding import Mesh, PartitionSpec as P

SQRT_TWO_OVER_PI = 0.7978845608028654
CUBIC = 0.044715
F32, BF16 = jnp.float32, jnp.bfloat16
SIZES = {"y": 4, "zl": 2, "co": 2, "zh": 4, "x": 4}
GROUPS = ((0,), (1, 3), (2,))


def shift(block, axis, step):
    n = SIZES[axis]
    return lax.ppermute(block, axis, [(i, (i + step) % n) for i in range(n)])


def turned(block, dim, start):
    twice = jnp.concatenate([block, block], axis=dim)
    return lax.dynamic_slice_in_dim(twice, start, block.shape[dim], axis=dim)


def activation(pre, grad_pre):
    inner = jnp.tanh(SQRT_TWO_OVER_PI * (pre + CUBIC * pre * pre * pre))
    value = 0.5 * pre * (1.0 + inner)
    slope = 0.5 * (1.0 + inner) + 0.5 * pre * (1.0 - inner * inner) * SQRT_TWO_OVER_PI * (
        1.0 + 3.0 * CUBIC * pre * pre
    )
    return value.astype(BF16), (grad_pre * slope).astype(BF16)


def add(*terms):
    total = terms[0].astype(F32)
    for term in terms[1:]:
        total = total + term.astype(F32)
    return total


def matmul(a, b, dims):
    return lax.dot_general(a, b, (dims, ((), ())), preferred_element_type=F32)


def row_sum(pre, grad):
    far_pre, far_grad = shift(pre[2], "y", 1), shift(grad[2], "y", -1)
    up = shift(jnp.stack([add(pre[1], far_pre).astype(BF16), grad[1]]), "y", 1)
    down = shift(jnp.stack([pre[3], add(grad[3], far_grad).astype(BF16)]), "y", -1)
    other = jnp.stack([add(pre[0, 1], up[0, 1], down[0, 1]), add(grad[0, 1], up[1, 1], down[1, 1])])
    other = shift(other.astype(BF16), "zl", 1)
    return (
        add(pre[0, 0], up[0, 0], down[0, 0], other[0]),
        add(grad[0, 0], up[1, 0], down[1, 0], other[1]),
    )


def row_gather(value, grad):
    own = jnp.stack([value, grad])
    pair = jnp.stack([own, shift(own, "zl", 1)], axis=1)
    prev, following = shift(pair, "y", 1), shift(pair, "y", -1)
    far_value, far_grad = shift(prev[0], "y", 1), shift(following[1], "y", -1)
    return (
        jnp.stack([pair[0], following[0], far_value, prev[0]]),
        jnp.stack([pair[1], following[1], far_grad, prev[1]]),
    )


def body(tokens, up_weight, down_weight, cotangent):
    core, y, zl = (lax.axis_index(name) for name in ("co", "y", "zl"))
    other_up, other_down = shift(up_weight, "co", 1), shift(down_weight, "co", 1)
    both = jnp.stack([tokens, cotangent]).reshape(2, 2, 4, 16, 384)
    both = turned(turned(both, 1, core), 2, y)
    shard = jnp.concatenate([both[:, 0], shift(both[:, 1], "co", 1)], axis=-1)
    up_full = jnp.concatenate([up_weight, other_up], axis=0)
    down_full = jnp.concatenate([down_weight, other_down], axis=1)

    before, after, across = shift(shard, "zh", 1), shift(shard, "zh", -1), shift(shard, "zh", 2)
    near = [
        jnp.where(zl == 0, shard, across),
        jnp.where(zl == 0, after, before),
        jnp.where(zl == 0, across, shard),
        jnp.where(zl == 0, before, after),
    ]
    near = jnp.stack(near, axis=2).reshape(2, 4, 2, 32, 768)
    before, after = shift(near, "x", 1), shift(near, "x", -1)
    across = jnp.stack([shift(before[0], "x", 1), shift(after[1], "x", -1)])
    blocks = {0: near, 1: after, 2: across, 3: before}

    taken, activated = [], []
    for group in GROUPS:
        inputs = jnp.concatenate([blocks[k] for k in group], axis=3)
        t = inputs.shape[3]
        token_part, cot_part = inputs[0].reshape(8 * t, 768), inputs[1].reshape(8 * t, 768)
        pre = matmul(token_part, up_full, ((1,), (0,))).astype(BF16).reshape(4, 2, t, 1536)
        grad = matmul(cot_part, down_full, ((1,), (1,))).astype(BF16).reshape(4, 2, t, 1536)
        taken.append((token_part, cot_part))
        activated.append(activation(*row_sum(pre, grad)))

    gathered, partial = [None] * len(GROUPS), {}
    for g in reversed(range(len(GROUPS))):
        value, grad = (a.reshape(-1, 1536) for a in row_gather(*activated[g]))
        gathered[g] = (value, grad)
        n = len(GROUPS[g])
        outs = jnp.stack(
            [
                matmul(value, down_full, ((1,), (0,))).astype(BF16),
                matmul(grad, up_full, ((1,), (1,))).astype(BF16),
            ]
        ).reshape(2, 8, n, 32, 768)
        for i, k in enumerate(GROUPS[g]):
            partial[k] = outs[:, :, i]

    far_out, far_grad = shift(partial[2][0], "x", 1), shift(partial[2][1], "x", -1)
    ahead = shift(jnp.stack([add(partial[1][0], far_out).astype(BF16), partial[1][1]]), "x", 1)
    back = shift(jnp.stack([partial[3][0], add(partial[3][1], far_grad).astype(BF16)]), "x", -1)
    mine = add(partial[0], ahead, back).reshape(2, 4, 4, 16, 768)
    first = [jnp.where(zl == 0, mine[:, :, i], mine[:, :, (i + 2) % 4]) for i in range(4)]
    summed = add(
        first[0],
        shift(first[1].astype(BF16), "zh", 1),
        shift(first[2].astype(BF16), "zh", 2),
        shift(first[3].astype(BF16), "zh", -1),
    ).astype(BF16)
    halves = jnp.stack([summed[..., :384], shift(summed[..., 384:], "co", 1)], axis=1)
    halves = halves.reshape(2, 2, 4, 16, 384)
    outs = turned(turned(halves, 1, core), 2, (4 - y) % 4).reshape(2, 128, 384)

    token_all, cot_all, value_all, grad_all = (
        jnp.concatenate([pair[i] for pair in pairs]) for pairs in (taken, gathered) for i in (0, 1)
    )
    other_up = shift(matmul(token_all[:, 384:], grad_all, ((0,), (0,))).astype(BF16), "co", 1)
    other_down = shift(matmul(value_all, cot_all[:, 384:], ((0,), (0,))).astype(BF16), "co", 1)
    up_grad = matmul(token_all[:, :384], grad_all, ((0,), (0,))) + other_up.astype(F32)
    down_grad = matmul(value_all, cot_all[:, :384], ((0,), (0,))) + other_down.astype(F32)
    return outs[0], outs[1], up_grad, down_grad


def solution(mesh):
    axes = tuple(SIZES)
    row, col = ("y", "zl", "co"), ("zh", "x")
    fine = Mesh(mesh.devices.reshape(tuple(SIZES.values())), axes)
    placed = (P(col, row), P(row, col), P(col, row), P(col, row))
    return jax.shard_map(
        body,
        mesh=fine,
        in_specs=placed,
        out_specs=(P(col, row), P(col, row), P(row, col), P(col, row)),
        check_vma=False,
    )
```

```python
import jax
import jax.numpy as jnp
from jax import lax
from jax.sharding import Mesh, PartitionSpec as P

SQRT_TWO_OVER_PI = 0.7978845608028654
CUBIC = 0.044715
F32, BF16 = jnp.float32, jnp.bfloat16
SIZES = {"y": 4, "zl": 2, "co": 2, "zh": 4, "x": 4}

def shift(block, axis, step):
    n = SIZES[axis]
    return lax.ppermute(block, axis, [(i, (i + step) % n) for i in range(n)])


def turned(block, dim, start):
    twice = jnp.concatenate([block, block], axis=dim)
    return lax.dynamic_slice_in_dim(twice, start, block.shape[dim], axis=dim)


def activation(pre, grad_pre):
    inner = jnp.tanh(SQRT_TWO_OVER_PI * (pre + CUBIC * pre * pre * pre))
    value = 0.5 * pre * (1.0 + inner)
    slope = 0.5 * (1.0 + inner) + 0.5 * pre * (1.0 - inner * inner) * SQRT_TWO_OVER_PI * (
        1.0 + 3.0 * CUBIC * pre * pre
    )
    return value.astype(BF16), (grad_pre * slope).astype(BF16)


def add(*terms):
    total = terms[0].astype(F32)
    for term in terms[1:]:
        total = total + term.astype(F32)
    return total


def matmul(a, b, dims):
    return lax.dot_general(a, b, (dims, ((), ())), preferred_element_type=F32)


def behind(blocks, *earlier):
    return lax.optimization_barrier((blocks, earlier))[0]


def chosen(swap, parts):
    return [jnp.where(swap, parts[(i + 2) % 4], parts[i]) for i in range(4)]


def body(tokens, up_weight, down_weight, cotangent):
    core, y, zl = (lax.axis_index(name) for name in ("co", "y", "zl"))
    swap = zl == 1
    both = jnp.stack([tokens, cotangent]).reshape(2, 2, 4, 16, 384)
    both = turned(turned(both, 1, core), 2, y)
    other_half = shift(both[:, 1], "co", 1)
    other_up, other_down = shift(up_weight, "co", 1), shift(down_weight, "co", 1)
    shard = jnp.concatenate([both[:, 0], other_half], axis=-1)

    def col_gather(block):
        return [block, shift(block, "x", -1), shift(block, "x", 2), shift(block, "x", 1)]

    def laid(parts):
        return jnp.stack(chosen(swap, parts), axis=2).reshape(2, 4, 2, -1, 768)

    def first_layers(block):
        t = block.shape[3]
        pre = matmul(block[0].reshape(8 * t, 768), up_full, ((1,), (0,))).astype(BF16)
        grad = matmul(block[1].reshape(8 * t, 768), down_full, ((1,), (1,))).astype(BF16)
        return pre.reshape(4, 2, t, 1536), grad.reshape(4, 2, t, 1536)

    def sum_one(pre, grad):
        return shift(pre[2], "y", 1), shift(grad[2], "y", -1)

    def sum_two(pre, grad, far):
        up = jnp.stack([add(pre[1], far[0]).astype(BF16), grad[1]])
        down = jnp.stack([pre[3], add(grad[3], far[1]).astype(BF16)])
        return up, down

    def sum_three(pre, grad, up, down):
        own = jnp.stack([add(pre[0], up[0], down[0]), add(grad[0], up[1], down[1])])
        return own[:, 0], own[:, 1].astype(BF16)

    def active(own, other):
        return jnp.stack(activation(own[0] + other[0].astype(F32), own[1] + other[1].astype(F32)))

    def gather_two(pair, prev, following):
        return shift(prev[0], "y", 1), shift(following[1], "y", -1)

    def rows(pair, prev, following, far):
        return (
            jnp.stack([pair[0], following[0], far[0], prev[0]]).reshape(-1, 1536),
            jnp.stack([pair[1], following[1], far[1], prev[1]]).reshape(-1, 1536),
        )

    def second_layers(value, grad):
        outs = jnp.stack(
            [
                matmul(value, down_full, ((1,), (0,))).astype(BF16),
                matmul(grad, up_full, ((1,), (1,))).astype(BF16),
            ]
        ).reshape(2, 4, 4, -1, 768)
        return chosen(swap, [outs[:, :, i] for i in range(4)])

    def col_send(parts):
        return [parts[0], shift(parts[1], "x", 1), shift(parts[2], "x", 2), shift(parts[3], "x", -1)]

    def flat(block, i):
        return block[i].reshape(-1, 768)

    up_full = jnp.concatenate([up_weight, other_up], axis=0)
    down_full = jnp.concatenate([down_weight, other_down], axis=1)
    shard = behind(shard, other_up, other_down)
    parts_a = col_gather(shard)
    after, before = shift(shard, "zh", -1), shift(shard, "zh", 1)

    in_a = laid(parts_a)
    pg_a = first_layers(in_a)
    far_a = sum_one(*pg_a)
    joined = behind(jnp.concatenate([after, before], axis=2), pg_a)
    parts_b = col_gather(joined)
    ud_a = sum_two(*behind(pg_a, joined), far_a)
    mid_a = (shift(ud_a[0], "y", 1), shift(ud_a[1], "y", -1))

    in_b = laid(behind(parts_b, ud_a))
    pg_b = first_layers(in_b)
    far_b = sum_one(*pg_b)
    across = shift(behind(shard, in_b), "zh", 2)
    own_a, send_a = sum_three(*behind(pg_a, pg_b), *mid_a)
    zl_a = shift(send_a, "zl", 1)
    ud_b = sum_two(*behind(pg_b, send_a), far_b)
    mid_b = (shift(ud_b[0], "y", 1), shift(ud_b[1], "y", -1))
    across = behind(across, ud_b)
    parts_c = col_gather(across)
    act_a = active(own_a, behind(zl_a, across))
    pair_a = jnp.stack([act_a, shift(act_a, "zl", 1)], axis=1)
    in_c = laid(behind(parts_c, pair_a))
    pg_c = first_layers(in_c)
    far_c = sum_one(*pg_c)
    own_b, send_b = sum_three(*behind(pg_b, pg_c), *mid_b)
    zl_b = shift(send_b, "zl", 1)
    ud_c = sum_two(*behind(pg_c, send_b), far_c)
    mid_c = (shift(ud_c[0], "y", 1), shift(ud_c[1], "y", -1))

    pair_a = behind(pair_a, ud_c)
    near_a = (shift(pair_a, "y", 1), shift(pair_a, "y", -1))
    act_b = active(own_b, behind(zl_b, pair_a))
    pair_b = jnp.stack([act_b, shift(act_b, "zl", 1)], axis=1)
    own_c, send_c = sum_three(*behind(pg_c, act_b), *mid_c)
    zl_c = shift(send_c, "zl", 1)
    far_a = gather_two(pair_a, *behind(near_a, send_c))
    pair_b = behind(pair_b, near_a)
    near_b = (shift(pair_b, "y", 1), shift(pair_b, "y", -1))
    act_c = active(own_c, behind(zl_c, pair_b))
    pair_c = jnp.stack([act_c, shift(act_c, "zl", 1)], axis=1)
    rows_a = rows(pair_a, *near_a, behind(far_a, act_c))
    outs_a = second_layers(*rows_a)
    pair_c = behind(pair_c, outs_a)
    near_c = (shift(pair_c, "y", 1), shift(pair_c, "y", -1))
    far_b = gather_two(pair_b, *behind(near_b, pair_c))
    far_c = gather_two(pair_c, *near_c)
    rows_b = rows(pair_b, *near_b, behind(far_b, near_c))
    outs_b = second_layers(*rows_b)
    sent_b = col_send([jnp.concatenate(parts, axis=2) for parts in zip(outs_a, outs_b)])

    first = ((0,), (0,))
    rows_c = rows(pair_c, *near_c, behind(far_c, outs_b))
    outs_c = second_layers(*rows_c)
    sent_c = col_send(outs_c)

    value_rest, grad_rest = behind(
        tuple(jnp.concatenate([rows_a[i], rows_b[i]]) for i in range(2)), outs_c
    )
    up_rest = matmul(jnp.concatenate([flat(in_a, 0), flat(in_b, 0)]), grad_rest, first)
    down_rest = matmul(value_rest, jnp.concatenate([flat(in_a, 1), flat(in_b, 1)]), first)
    sum_b = add(*behind(sent_b, up_rest, down_rest)).reshape(2, 4, 3, 16, 768)
    from_1 = shift(sum_b[:, :, 1].astype(BF16), "zh", 1)
    from_3 = shift(sum_b[:, :, 2].astype(BF16), "zh", -1)
    sum_c = add(*behind(sent_c, sum_b)).astype(BF16).reshape(2, 4, 16, 768)
    from_2 = shift(sum_c, "zh", 2)
    value_c, grad_c = behind(rows_c, sum_c)
    token_c, cot_c = flat(in_c, 0), flat(in_c, 1)
    up_there = (up_rest[384:] + matmul(token_c[:, 384:], grad_c, first)).astype(BF16)
    down_there = (down_rest[:, 384:] + matmul(value_c, cot_c[:, 384:], first)).astype(BF16)
    other_up, other_down = shift(up_there, "co", 1), shift(down_there, "co", 1)

    value_c, grad_c = behind((value_c, grad_c), up_there, down_there)
    up_grad = up_rest[:384] + matmul(token_c[:, :384], grad_c, first)
    down_grad = down_rest[:, :384] + matmul(value_c, cot_c[:, :384], first)
    up_grad = up_grad + other_up.astype(F32)
    down_grad = down_grad + other_down.astype(F32)
    last = lax.optimization_barrier(((from_1, from_3, from_2), (up_grad, down_grad)))
    (from_1, from_3, from_2), (up_grad, down_grad) = last

    summed = add(sum_b[:, :, 0], from_1, from_3, from_2).astype(BF16)
    far_half = shift(summed[..., 384:], "co", 1)
    halves = jnp.stack([summed[..., :384], far_half], axis=1)
    outs = turned(turned(halves, 1, core), 2, (4 - y) % 4).reshape(2, 128, 384)
    return outs[0], outs[1], up_grad, down_grad


def solution(mesh):
    axes = tuple(SIZES)
    row, col = ("y", "zl", "co"), ("zh", "x")
    fine = Mesh(mesh.devices.reshape(tuple(SIZES.values())), axes)
    placed = (P(col, row), P(row, col), P(col, row), P(col, row))
    return jax.shard_map(
        body,
        mesh=fine,
        in_specs=placed,
        out_specs=(P(col, row), P(col, row), P(row, col), P(col, row)),
        check_vma=False,
    )
```

```python
import jax
import jax.numpy as jnp
from jax import lax
from jax.sharding import Mesh, PartitionSpec as P

SQRT_TWO_OVER_PI = 0.7978845608028654
CUBIC = 0.044715
F32, BF16 = jnp.float32, jnp.bfloat16
SIZES = {"y": 4, "zl": 2, "co": 2, "zh": 4, "x": 4}

def shift(block, axis, step):
    n = SIZES[axis]
    return lax.ppermute(block, axis, [(i, (i + step) % n) for i in range(n)])


def turned(block, dim, start):
    twice = jnp.concatenate([block, block], axis=dim)
    return lax.dynamic_slice_in_dim(twice, start, block.shape[dim], axis=dim)


def activation(pre, grad_pre):
    inner = jnp.tanh(SQRT_TWO_OVER_PI * (pre + CUBIC * pre * pre * pre))
    value = 0.5 * pre * (1.0 + inner)
    slope = 0.5 * (1.0 + inner) + 0.5 * pre * (1.0 - inner * inner) * SQRT_TWO_OVER_PI * (
        1.0 + 3.0 * CUBIC * pre * pre
    )
    return value.astype(BF16), (grad_pre * slope).astype(BF16)


def add(*terms):
    total = terms[0].astype(F32)
    for term in terms[1:]:
        total = total + term.astype(F32)
    return total


def matmul(a, b, dims):
    return lax.dot_general(a, b, (dims, ((), ())), preferred_element_type=F32)


def behind(blocks, *earlier):
    return lax.optimization_barrier((blocks, earlier))[0]


def chosen(swap, parts):
    return [jnp.where(swap, parts[(i + 2) % 4], parts[i]) for i in range(4)]


def body(tokens, up_weight, down_weight, cotangent):
    core, y, zl = (lax.axis_index(name) for name in ("co", "y", "zl"))
    swap = zl == 1
    both = jnp.stack([tokens, cotangent]).reshape(2, 2, 4, 16, 384)
    both = turned(turned(both, 1, core), 2, y)
    other_half = shift(both[:, 1], "co", 1)
    other_up, other_down = shift(up_weight, "co", 1), shift(down_weight, "co", 1)
    shard = jnp.concatenate([both[:, 0], other_half], axis=-1)

    def col_gather(block):
        return [block, shift(block, "x", -1), shift(block, "x", 2), shift(block, "x", 1)]

    def laid(parts):
        return jnp.stack(chosen(swap, parts), axis=2).reshape(2, 4, 2, -1, 768)

    def first_layers(block):
        t = block.shape[3]
        pre = matmul(block[0].reshape(8 * t, 768), up_full, ((1,), (0,))).astype(BF16)
        grad = matmul(block[1].reshape(8 * t, 768), down_full, ((1,), (1,))).astype(BF16)
        return pre.reshape(4, 2, t, 1536), grad.reshape(4, 2, t, 1536)

    def sum_one(pre, grad):
        return shift(pre[2], "y", 1), shift(grad[2], "y", -1)

    def sum_two(pre, grad, far):
        up = jnp.stack([add(pre[1], far[0]).astype(BF16), grad[1]])
        down = jnp.stack([pre[3], add(grad[3], far[1]).astype(BF16)])
        return up, down

    def sum_three(pre, grad, up, down):
        own = jnp.stack([add(pre[0], up[0], down[0]), add(grad[0], up[1], down[1])])
        return own[:, 0], own[:, 1].astype(BF16)

    def active(own, other):
        return jnp.stack(activation(own[0] + other[0].astype(F32), own[1] + other[1].astype(F32)))

    def gather_two(pair, prev, following):
        return shift(prev[0], "y", 1), shift(following[1], "y", -1)

    def rows(pair, prev, following, far):
        return (
            jnp.stack([pair[0], following[0], far[0], prev[0]]).reshape(-1, 1536),
            jnp.stack([pair[1], following[1], far[1], prev[1]]).reshape(-1, 1536),
        )

    def second_layers(value, grad):
        outs = jnp.stack(
            [
                matmul(value, down_full, ((1,), (0,))).astype(BF16),
                matmul(grad, up_full, ((1,), (1,))).astype(BF16),
            ]
        ).reshape(2, 4, 4, -1, 768)
        return chosen(swap, [outs[:, :, i] for i in range(4)])

    def col_send(parts):
        return [parts[0], shift(parts[1], "x", 1), shift(parts[2], "x", 2), shift(parts[3], "x", -1)]

    def flat(block, i):
        return block[i].reshape(-1, 768)

    up_full = jnp.concatenate([up_weight, other_up], axis=0)
    down_full = jnp.concatenate([down_weight, other_down], axis=1)
    shard = behind(shard, other_up, other_down)
    parts_a = col_gather(shard)
    after, before = shift(shard, "zh", -1), shift(shard, "zh", 1)

    in_a = laid(parts_a)
    pg_a = first_layers(in_a)
    far_a = sum_one(*pg_a)
    joined = behind(jnp.concatenate([after, before], axis=2), pg_a)
    parts_b = col_gather(joined)
    ud_a = sum_two(*behind(pg_a, joined), far_a)
    mid_a = (shift(ud_a[0], "y", 1), shift(ud_a[1], "y", -1))

    in_b = laid(behind(parts_b, ud_a))
    pg_b = first_layers(in_b)
    far_b = sum_one(*pg_b)
    across = shift(behind(shard, in_b), "zh", 2)
    own_a, send_a = sum_three(*behind(pg_a, pg_b), *mid_a)
    zl_a = shift(send_a, "zl", 1)
    ud_b = sum_two(*behind(pg_b, send_a), far_b)
    mid_b = (shift(ud_b[0], "y", 1), shift(ud_b[1], "y", -1))
    across = behind(across, ud_b)
    parts_c = col_gather(across)
    act_a = active(own_a, behind(zl_a, across))
    pair_a = jnp.stack([act_a, shift(act_a, "zl", 1)], axis=1)
    in_c = laid(behind(parts_c, pair_a))
    pg_c = first_layers(in_c)
    far_c = sum_one(*pg_c)
    own_b, send_b = sum_three(*behind(pg_b, pg_c), *mid_b)
    zl_b = shift(send_b, "zl", 1)
    ud_c = sum_two(*behind(pg_c, send_b), far_c)
    mid_c = (shift(ud_c[0], "y", 1), shift(ud_c[1], "y", -1))

    pair_a = behind(pair_a, ud_c)
    near_a = (shift(pair_a, "y", 1), shift(pair_a, "y", -1))
    act_b = active(own_b, behind(zl_b, pair_a))
    pair_b = jnp.stack([act_b, shift(act_b, "zl", 1)], axis=1)
    own_c, send_c = sum_three(*behind(pg_c, act_b), *mid_c)
    zl_c = shift(send_c, "zl", 1)
    far_a = gather_two(pair_a, *behind(near_a, send_c))
    pair_b = behind(pair_b, near_a)
    near_b = (shift(pair_b, "y", 1), shift(pair_b, "y", -1))
    act_c = active(own_c, behind(zl_c, pair_b))
    pair_c = jnp.stack([act_c, shift(act_c, "zl", 1)], axis=1)
    rows_a = rows(pair_a, *near_a, behind(far_a, act_c))
    outs_a = second_layers(*rows_a)
    pair_c = behind(pair_c, outs_a)
    near_c = (shift(pair_c, "y", 1), shift(pair_c, "y", -1))
    far_b = gather_two(pair_b, *behind(near_b, pair_c))
    far_c = gather_two(pair_c, *near_c)
    rows_b = rows(pair_b, *near_b, behind(far_b, near_c))
    outs_b = second_layers(*rows_b)
    first = ((0,), (0,))
    rows_c = rows(pair_c, *near_c, behind(far_c, outs_b))
    outs_c = second_layers(*rows_c)
    sent = col_send([jnp.concatenate(parts, axis=2) for parts in zip(outs_a, outs_b, outs_c)])

    value_rest, grad_rest = behind(
        tuple(jnp.concatenate([rows_a[i], rows_b[i]]) for i in range(2)), outs_c
    )
    up_rest = matmul(jnp.concatenate([flat(in_a, 0), flat(in_b, 0)]), grad_rest, first)
    down_rest = matmul(value_rest, jnp.concatenate([flat(in_a, 1), flat(in_b, 1)]), first)
    sum_b = add(*behind(sent, up_rest, down_rest)).reshape(2, 4, 4, 16, 768)
    from_1 = shift(sum_b[:, :, 1].astype(BF16), "zh", 1)
    from_3 = shift(sum_b[:, :, 2].astype(BF16), "zh", -1)
    from_2 = shift(sum_b[:, :, 3].astype(BF16), "zh", 2)
    value_c, grad_c = behind(rows_c, sum_b)
    token_c, cot_c = flat(in_c, 0), flat(in_c, 1)
    up_there = (up_rest[384:] + matmul(token_c[:, 384:], grad_c, first)).astype(BF16)
    down_there = (down_rest[:, 384:] + matmul(value_c, cot_c[:, 384:], first)).astype(BF16)
    other_up, other_down = shift(up_there, "co", 1), shift(down_there, "co", 1)

    value_c, grad_c = behind((value_c, grad_c), up_there, down_there)
    up_grad = up_rest[:384] + matmul(token_c[:, :384], grad_c, first)
    down_grad = down_rest[:, :384] + matmul(value_c, cot_c[:, :384], first)
    up_grad = up_grad + other_up.astype(F32)
    down_grad = down_grad + other_down.astype(F32)
    last = lax.optimization_barrier(((from_1, from_3, from_2), (up_grad, down_grad)))
    (from_1, from_3, from_2), (up_grad, down_grad) = last

    summed = add(sum_b[:, :, 0], from_1, from_3, from_2).astype(BF16)
    far_half = shift(summed[..., 384:], "co", 1)
    halves = jnp.stack([summed[..., :384], far_half], axis=1)
    outs = turned(turned(halves, 1, core), 2, (4 - y) % 4).reshape(2, 128, 384)
    return outs[0], outs[1], up_grad, down_grad


def solution(mesh):
    axes = tuple(SIZES)
    row, col = ("y", "zl", "co"), ("zh", "x")
    fine = Mesh(mesh.devices.reshape(tuple(SIZES.values())), axes)
    placed = (P(col, row), P(row, col), P(col, row), P(col, row))
    return jax.shard_map(
        body,
        mesh=fine,
        in_specs=placed,
        out_specs=(P(col, row), P(col, row), P(row, col), P(col, row)),
        check_vma=False,
    )
```
